32 devices in a mesh: slab: 4 (over z), inner: 8 (over y, x, core).
Axes of the slice: x: 2, y: 2, z: 4, core: 2. Of those that a mesh axis runs over, the one named last changes fastest.
Arguments:
- coords_fine: float32 [3, 32768], P(None, ('slab', 'inner')), may hold values from 0 to 1, as said below
- coords_coarse: float32 [3, 131072], P(None, 'slab'), may hold values from 0 to 1, as said below
- set_index: int32 [4, 16, 8, 512], P('slab', None, 'inner'), may hold values from 0 to 106495, as said below
- counts: int32 [4, 16, 8], P('slab', None, 'inner'), may hold values from 128 to 512
- morton_slot: int32 [4, 16, 8], P('slab', None, 'inner'), may hold values from 0 to 127, as said below
Outputs:
- factor_blocks: float32 [4, 8, 16, 64, 512], P('slab', 'inner')
The draws below stay inside these ranges and needn't reach their ends.
Inputs may be any that keep to these rules, and one draw needn't show every extreme that they name: `coords_fine`: x and y lie in [0, 1]; the z of a point of slab b lies in [b / 4, (b + 1) / 4]. `coords_coarse`: x and y lie in [0, 1]; the z of a point of slab b lies in [b / 4, (b + 1) / 4]. `set_index`: every entry names a finest-level point of the supernode's own slab or a coarse-level point of its own slab or of a slab directly beside it (never a slab outside 0 to 4 - 1); the last 64 entries are the supernode's own points, and every finest-level point of a slab is the own point of exactly one of its supernodes. `morton_slot`: in each slab every place occurs once; at most 2 supernodes of one device have places of one owner (place // 16), and this most is reached.
All inputs are finite; a program needn't handle non-finite values.
Results may differ from the reference program's by a relative error of at most 0.0003.
Values sent between devices are 32-bit elements; how exact they have to be, the bound alone decides.
A program may use at most 320 MiB of HBM per device.

```python
import math
import jax
import jax.numpy as jnp
from jax import lax

MEMB = 64
P_SIZE = 512
SN_DEV = 16
COARSE_SLAB = 32768
FINE_SLAB = 8192
NFINE = 32768
NCOARSE = 131072
N_SLAB = 4
N_INNER = 8


def place_points(key, total, per_slab):
    unit = jax.random.uniform(key, (3, total), jnp.float32)
    slabs = total // per_slab
    which = (jnp.arange(total, dtype=jnp.int32) // per_slab).astype(jnp.float32)
    depth = (which + unit[2]) / slabs
    return jnp.stack([unit[0], unit[1], depth], axis=0).astype(jnp.float32)


def draw_coords_fine(key, part):
    return place_points(jax.random.fold_in(key, 11), NFINE, FINE_SLAB)


def draw_coords_coarse(key, part):
    return place_points(jax.random.fold_in(key, 12), NCOARSE, COARSE_SLAB)


def draw_set_index(key, part):
    key_perm, key_fine, key_coarse, key_pick, key_region = jax.random.split(jax.random.fold_in(key, 13), 5)
    perms = jax.vmap(lambda k: jax.random.permutation(k, FINE_SLAB))(jax.random.split(key_perm, N_SLAB))
    members = perms.astype(jnp.int32).reshape(N_SLAB, SN_DEV, N_INNER, MEMB)
    others_shape = (N_SLAB, SN_DEV, N_INNER, P_SIZE - MEMB)
    slab_ids = jnp.arange(N_SLAB, dtype=jnp.int32)[:, None, None, None]
    low = (slab_ids == 0).astype(jnp.int32)
    high = 3 - (slab_ids == N_SLAB - 1).astype(jnp.int32)
    region = jax.random.randint(key_region, others_shape, jnp.broadcast_to(low, others_shape), jnp.broadcast_to(high, others_shape), dtype=jnp.int32)
    fine_pick = jax.random.randint(key_fine, others_shape, 0, FINE_SLAB, dtype=jnp.int32)
    coarse_pick = FINE_SLAB + region * COARSE_SLAB + jax.random.randint(key_coarse, others_shape, 0, COARSE_SLAB, dtype=jnp.int32)
    chooser = jax.random.randint(key_pick, others_shape, 0, 4, dtype=jnp.int32)
    others = jnp.where(chooser == 0, coarse_pick, fine_pick)
    return jnp.concatenate([others, members], axis=-1).astype(jnp.int32)


def draw_morton_slot(key, part):
    capacity = max(1, SN_DEV // N_INNER)
    key_off, key_owner, key_spot = jax.random.split(jax.random.fold_in(key, 14), 3)
    offsets = jax.vmap(lambda k: jax.random.permutation(k, N_INNER))(jax.random.split(key_off, N_SLAB)).astype(jnp.int32)
    relabel = jax.vmap(lambda k: jax.random.permutation(k, N_INNER))(jax.random.split(key_owner, N_SLAB)).astype(jnp.int32)
    spots = jax.vmap(lambda k: jax.random.permutation(k, SN_DEV))(jax.random.split(key_spot, N_SLAB * N_INNER)).astype(jnp.int32)
    spots = spots.reshape(N_SLAB, N_INNER, SN_DEV)
    local = jnp.arange(SN_DEV, dtype=jnp.int32)
    source = jnp.arange(N_INNER, dtype=jnp.int32)
    group_off = offsets[:, local // capacity]
    raw_owner = (group_off[:, :, None] + source[None, None, :]) % N_INNER
    owner = jnp.take_along_axis(relabel, raw_owner.reshape(N_SLAB, -1), axis=1).reshape(N_SLAB, SN_DEV, N_INNER)
    slab_ids = jnp.broadcast_to(jnp.arange(N_SLAB, dtype=jnp.int32)[:, None, None], owner.shape)
    local_ids = jnp.broadcast_to(local[None, :, None], owner.shape)
    spot = spots[slab_ids, owner, local_ids]
    return (owner * SN_DEV + spot).astype(jnp.int32)


def set_ends(entries, key, least, high):
    index_at = [jax.random.randint(jax.random.fold_in(key, axis), (), 0, length) for axis, length in enumerate(entries.shape)]
    main_axis = entries.shape.index(max(entries.shape))
    next_to = index_at[:main_axis] + [(index_at[main_axis] + 1) % entries.shape[main_axis]] + index_at[main_axis + 1:]
    return entries.at[tuple(index_at)].set(least).at[tuple(next_to)].set(high)


def setup_inputs(seed: int = 0) -> dict:
    keys = jax.random.split(jax.random.key(seed), 6)
    coords_fine = draw_coords_fine(jax.random.fold_in(keys[5], 71), 0)
    coords_coarse = draw_coords_coarse(jax.random.fold_in(keys[5], 71), 0)
    set_index = draw_set_index(jax.random.fold_in(keys[5], 71), 0)
    counts = set_ends(jax.random.randint(keys[3], (N_SLAB, SN_DEV, N_INNER), 2 * MEMB, P_SIZE + 1), jax.random.fold_in(keys[3], 1), 2 * MEMB, P_SIZE).astype(jnp.int32)
    morton_slot = draw_morton_slot(jax.random.fold_in(keys[5], 71), 0)
    return {"coords_fine": coords_fine, "coords_coarse": coords_coarse, "set_index": set_index, "counts": counts, "morton_slot": morton_slot}


LENGTH_SCALE = 0.2
NUGGET = 0.5

def factor_one(points, count):
    width = points.shape[1]
    diffs = points[:, :, None] - points[:, None, :]
    dist = jnp.sqrt(lax.optimization_barrier(jnp.sum(diffs * diffs, axis=0))) * (math.sqrt(3.0) / LENGTH_SCALE)
    kern = (1.0 + dist) * jnp.exp(-dist)
    position = jnp.arange(width, dtype=jnp.int32)
    valid = (position >= width - count).astype(jnp.float32)
    diag_term = valid * NUGGET + (1.0 - valid)
    kernel = kern * valid[:, None] * valid[None, :] + jnp.diag(diag_term)
    chol = jnp.linalg.cholesky(kernel)
    member = jnp.arange(MEMB, dtype=jnp.int32)
    picks = (position[:, None] == (width - MEMB + member)[None, :]).astype(jnp.float32)
    solved = jax.scipy.linalg.solve_triangular(chol, picks, lower=True, trans=1)
    return solved.T

def reference(coords_fine, coords_coarse, set_index, counts, morton_slot):
    width = set_index.shape[-1]
    nslab = set_index.shape[0]
    per_slab = set_index.shape[1] * set_index.shape[2]
    fine_slab = coords_fine.shape[1] // nslab
    coarse_slab = coords_coarse.shape[1] // nslab
    slab_of = jnp.repeat(jnp.arange(nslab, dtype=jnp.int32), per_slab)
    flat_index = set_index.reshape(-1, width).astype(jnp.int32)
    flat_count = counts.reshape(-1).astype(jnp.int32)

    def one(item):
        wanted, count, slab = item
        fine_col = jnp.clip(wanted + slab * fine_slab, 0, coords_fine.shape[1] - 1).astype(jnp.int32)
        coarse_col = jnp.clip(wanted - fine_slab + (slab - 1) * coarse_slab, 0, coords_coarse.shape[1] - 1).astype(jnp.int32)
        fine_pts = jnp.take(coords_fine, fine_col, axis=1)
        coarse_pts = jnp.take(coords_coarse, coarse_col, axis=1)
        points = jnp.where((wanted < fine_slab)[None, :], fine_pts, coarse_pts)
        return factor_one(points, count)
    blocks = lax.map(one, (flat_index, flat_count, slab_of))
    blocks = blocks.reshape(nslab, per_slab, MEMB, width)
    places = morton_slot.reshape(nslab, per_slab).astype(jnp.int32)
    slab_ids = jnp.broadcast_to(jnp.arange(nslab, dtype=jnp.int32)[:, None], (nslab, per_slab))
    ordered = jnp.zeros((nslab, per_slab, MEMB, width), jnp.float32)
    ordered = ordered.at[slab_ids, places].set(blocks)
    return ordered.reshape(nslab, set_index.shape[2], set_index.shape[1], MEMB, width)
```

```python
import math

import jax
import jax.numpy as jnp
from jax import lax
from jax.experimental import pallas as pl
from jax.experimental.pallas import tpu as pltpu
from jax.sharding import PartitionSpec as P

MEMB = 64
LENGTH_SCALE = 0.2
NUGGET = 0.5
LANES = 128
F32 = jnp.float32
BF16 = jnp.bfloat16


def split(x):
    high = x.astype(BF16)
    return high, (x - high.astype(F32)).astype(BF16)


def dot(a, b, dims=((1,), (0,))):
    return lax.dot_general(a, b, (dims, ((), ())), preferred_element_type=F32)


def dot3(a, b, dims=((1,), (0,))):
    ah, al = split(a)
    bh, bl = split(b)
    return dot(ah, bh, dims) + (dot(ah, bl, dims) + dot(al, bh, dims))


def gather_points(table_ref, index_ref, pts_ref, nsn, width):
    lane = lax.broadcasted_iota(jnp.int32, (8, LANES), 1)
    chunks = width // LANES

    def chunk(n, _):
        s = n // chunks
        c = n % chunks
        acc = jnp.zeros((8, LANES), F32)
        for p in range(LANES):
            number = index_ref[s, c * LANES + p]
            start = pl.multiple_of((number >> 7) * LANES, LANES)
            tile = table_ref[:, pl.ds(start, LANES)]
            tile = pltpu.roll(tile, (p - number) & (LANES - 1), 1)
            acc = jnp.where(lane == p, tile, acc)
        pts_ref[s, :, pl.ds(pl.multiple_of(c * LANES, LANES), LANES)] = acc
        return 0

    lax.fori_loop(0, nsn * chunks, chunk, 0)


def build_kernels(count_ref, pts_ref, k_ref, nsn, width):
    step = 64

    def one(s, _):
        first = width - count_ref[s]
        rows = pts_ref[s]
        cols = jnp.transpose(rows)
        for r in range(width // step):
            lo = r * step
            base = lo // LANES * LANES
            wide = width - base
            square = None
            for c in range(3):
                diff = cols[lo : lo + step, c : c + 1] - rows[c : c + 1, base:]
                square = diff * diff if square is None else square + diff * diff
            dist = jnp.sqrt(square) * (math.sqrt(3.0) / LENGTH_SCALE)
            kern = (1.0 + dist) * jnp.exp(-dist)
            p = lo + lax.broadcasted_iota(jnp.int32, (step, wide), 0)
            q = base + lax.broadcasted_iota(jnp.int32, (step, wide), 1)
            kern = jnp.where(jnp.minimum(p, q) >= first, kern, 0.0)
            kern = kern + jnp.where(p == q, jnp.where(p >= first, NUGGET, 1.0), 0.0)
            k_ref[s, lo : lo + step, base:] = kern
        return 0

    lax.fori_loop(0, nsn, one, 0)


def leaf(k_ref, work_ref, inv_ref, t, nsn):
    row = lax.broadcasted_iota(jnp.int32, (MEMB, LANES), 0)
    lane = lax.broadcasted_iota(jnp.int32, (MEMB, LANES), 1)
    lane_one = lax.broadcasted_iota(jnp.int32, (1, LANES), 1)
    lo = t * MEMB
    base = lo // LANES * LANES
    eye = (row + MEMB == lane).astype(F32)

    def load(s, _):
        tile = k_ref[s, lo : lo + MEMB, base : base + LANES]
        if lo != base:
            tile = pltpu.roll(tile, MEMB, 1)
        work_ref[s] = jnp.where(lane < MEMB, tile, eye)
        return 0

    lax.fori_loop(0, nsn, load, 0)

    for half in range(2):
        top = half * (MEMB // 2)
        tall = MEMB - top

        def pivot(k, _):
            hit = lane[:tall] == k
            below = row[:tall] + top > k
            for s in range(nsn):
                full = work_ref[s, top:]
                now = work_ref[s, pl.ds(k, 1), :]
                piv = jnp.sum(jnp.where(lane_one == k, now, 0.0), axis=1, keepdims=True)
                col = jnp.sum(jnp.where(hit, full, 0.0), axis=1, keepdims=True)
                work_ref[s, top:] = full - jnp.where(below, col, 0.0) * (now / piv)
            return 0

        lax.fori_loop(top, top + MEMB // 2, pivot, 0)

    def finish(s, _):
        full = work_ref[s]
        diag = jnp.sum(jnp.where(row == lane, full, 0.0), axis=1, keepdims=True)
        inv_ref[t, s] = pltpu.roll(full, MEMB, 1)[:, :MEMB] * lax.rsqrt(diag)
        return 0

    lax.fori_loop(0, nsn, finish, 0)


def update(k_ref, inv_ref, t, nsn, width):
    lo = t * MEMB
    after = lo + MEMB
    base = after // LANES * LANES

    def one(n, _):
        for u in range(2):
            s = n * 2 + u
            rows = dot3(inv_ref[t, s], k_ref[s, lo:after, base:])
            k_ref[s, lo:after, base:] = rows
            high, low = split(rows)
            left = jnp.concatenate([high, low, high], axis=0)
            right = jnp.concatenate([high, high, low], axis=0)
            for r in range(base, width, LANES):
                piece = dot(left[:, r - base : r - base + LANES], right[:, r - base :], ((0,), (0,)))
                k_ref[s, r : r + LANES, r:] = k_ref[s, r : r + LANES, r:] - piece
        return 0

    def one_half(n, _):
        for u in range(2):
            s = n * 2 + u
            rows = dot3(inv_ref[t, s], k_ref[s, lo:after, base:])
            high, low = split(rows)
            left = jnp.concatenate([high, low, high], axis=0)
            right = jnp.concatenate([high, high, low], axis=0)
            for r in range(base, width, LANES):
                piece = dot(left[:, r - base : r - base + LANES], right[:, r - base :], ((0,), (0,)))
                skip = MEMB if r == base else 0
                k_ref[s, r + skip : r + LANES, r:] = k_ref[s, r + skip : r + LANES, r:] - piece[skip:]
            k_ref[s, lo:after, base:] = rows
        return 0

    lax.fori_loop(0, nsn // 2, one if base == after else one_half, 0)


def back(k_ref, inv_ref, target_ref, out_ref, rest_ref, nsn, width):
    stages = width // MEMB

    def one(n, _):
        for u in range(2):
            s = n * 2 + u
            now = jnp.transpose(inv_ref[stages - 1, s])
            rest_ref[u, width - MEMB :] = now
            for j in range(stages - 1, 0, -1):
                lo = j * MEMB
                piece = dot3(k_ref[s, :lo, lo : lo + MEMB], now)
                if j == stages - 1:
                    rest_ref[u, :lo] = -piece
                else:
                    rest_ref[u, :lo] = rest_ref[u, :lo] - piece
                now = dot3(inv_ref[j - 1, s], rest_ref[u, lo - MEMB : lo], ((0,), (0,)))
                rest_ref[u, lo - MEMB : lo] = now
            out_ref[target_ref[s]] = jnp.transpose(rest_ref[u])
        return 0

    lax.fori_loop(0, nsn // 2, one, 0)


def factor_kernel(index_ref, count_ref, target_ref, table_ref, out_ref, pts_ref, k_ref, work_ref, inv_ref, rest_ref):
    nsn, width = index_ref.shape
    stages = width // MEMB
    gather_points(table_ref, index_ref, pts_ref, nsn, width)
    build_kernels(count_ref, pts_ref, k_ref, nsn, width)
    for t in range(stages):
        leaf(k_ref, work_ref, inv_ref, t, nsn)
        if t < stages - 1:
            update(k_ref, inv_ref, t, nsn, width)
    back(k_ref, inv_ref, target_ref, out_ref, rest_ref, nsn, width)


def factor_all(table, wanted, count, target, slots):
    nsn, width = wanted.shape
    smem = pl.BlockSpec(memory_space=pltpu.SMEM)
    vmem = pl.BlockSpec(memory_space=pltpu.VMEM)
    return pl.pallas_call(
        factor_kernel,
        out_shape=jax.ShapeDtypeStruct((slots, MEMB, width), F32),
        in_specs=[smem, smem, smem, vmem],
        out_specs=vmem,
        scratch_shapes=[
            pltpu.VMEM((nsn, 8, width), F32),
            pltpu.VMEM((nsn, width, width), F32),
            pltpu.VMEM((nsn, MEMB, LANES), F32),
            pltpu.VMEM((width // MEMB, nsn, MEMB, MEMB), F32),
            pltpu.VMEM((2, width, MEMB), F32),
        ],
        compiler_params=pltpu.CompilerParams(vmem_limit_bytes=50 * 1024 * 1024),
        name="factor",
    )(wanted, count, target, table)


def place_kernel(spot_ref, got_ref, out_ref, sems):
    nlocal = out_ref.shape[0]
    for i in range(got_ref.shape[0]):
        @pl.when(spot_ref[i] < nlocal)
        def _():
            pltpu.make_async_copy(got_ref.at[i], out_ref.at[spot_ref[i]], sems.at[i]).start()
    for i in range(got_ref.shape[0]):
        @pl.when(spot_ref[i] < nlocal)
        def _():
            pltpu.make_async_copy(got_ref.at[i], out_ref.at[spot_ref[i]], sems.at[i]).wait()


def place_all(got, spot, nlocal):
    return pl.pallas_call(
        place_kernel,
        out_shape=jax.ShapeDtypeStruct((nlocal,) + got.shape[1:], F32),
        in_specs=[pl.BlockSpec(memory_space=pltpu.SMEM), pl.BlockSpec(memory_space=pl.ANY)],
        out_specs=pl.BlockSpec(memory_space=pl.ANY),
        scratch_shapes=[pltpu.SemaphoreType.DMA((got.shape[0],))],
        name="place",
    )(spot, got)


def body(coords_fine, coords_coarse, set_index, counts, morton_slot):
    width = set_index.shape[-1]
    ends = lax.axis_size("slab") - 1
    fine = lax.all_gather(coords_fine, "inner", axis=1, tiled=True)
    below = lax.ppermute(coords_coarse, "slab", [(i, i + 1) for i in range(ends)])
    above = lax.ppermute(coords_coarse, "slab", [(i + 1, i) for i in range(ends)])
    table = jnp.concatenate([fine, below, coords_coarse, above], axis=1)
    table = jnp.pad(table, ((0, 5), (0, 0)))
    wanted = set_index.reshape(-1, width)
    count_here = counts.reshape(-1)
    places = morton_slot.reshape(-1)
    nlocal = wanted.shape[0]
    peers = lax.axis_size("inner")
    capacity = max(1, nlocal // peers)
    slots = peers * capacity
    owner = places // nlocal
    spot = places % nlocal
    order = jnp.arange(nlocal, dtype=jnp.int32)
    earlier = (owner[:, None] == owner[None, :]) & (order[None, :] < order[:, None])
    target = owner * capacity + jnp.sum(earlier.astype(jnp.int32), axis=1)
    hits = target[None, :] == jnp.arange(slots, dtype=jnp.int32)[:, None]
    send_spot = nlocal + jnp.sum(jnp.where(hits, spot[None, :] - nlocal, 0), axis=1)
    got_spot = lax.all_to_all(send_spot, "inner", split_axis=0, concat_axis=0, tiled=True)
    blocks = factor_all(table, wanted, count_here, target, slots)
    got_blocks = lax.all_to_all(blocks, "inner", split_axis=0, concat_axis=0, tiled=True)
    result = place_all(got_blocks, got_spot, nlocal)
    return result.reshape(1, 1, nlocal, MEMB, width)


def solution(mesh):
    placed = (
        P(None, ("slab", "inner")),
        P(None, "slab"),
        P("slab", None, "inner", None),
        P("slab", None, "inner"),
        P("slab", None, "inner"),
    )
    return jax.shard_map(
        body,
        mesh=mesh,
        in_specs=placed,
        out_specs=P("slab", "inner", None, None, None),
        check_vma=False,
    )
```

```python
import math

import jax
import jax.numpy as jnp
from jax import lax
from jax.experimental import pallas as pl
from jax.experimental.pallas import tpu as pltpu
from jax.sharding import PartitionSpec as P

MEMB = 64
LENGTH_SCALE = 0.2
NUGGET = 0.5
LANES = 128
F32 = jnp.float32
BF16 = jnp.bfloat16


def split(x):
    high = x.astype(BF16)
    return high, (x - high.astype(F32)).astype(BF16)


def dot(a, b, dims=((1,), (0,))):
    return lax.dot_general(a, b, (dims, ((), ())), preferred_element_type=F32)


def dot3(a, b, dims=((1,), (0,))):
    ah, al = split(a)
    bh, bl = split(b)
    return dot(ah, bh, dims) + (dot(ah, bl, dims) + dot(al, bh, dims))


def gather_points(table_ref, index_ref, pts_ref, nsn, width):
    lane = lax.broadcasted_iota(jnp.int32, (8, LANES), 1)
    chunks = width // LANES

    def chunk(n, _):
        s = n // chunks
        c = n % chunks
        acc = jnp.zeros((8, LANES), F32)
        for p in range(LANES):
            number = index_ref[s, c * LANES + p]
            start = pl.multiple_of((number >> 7) * LANES, LANES)
            tile = table_ref[:, pl.ds(start, LANES)]
            tile = pltpu.roll(tile, (p - number) & (LANES - 1), 1)
            acc = jnp.where(lane == p, tile, acc)
        pts_ref[s, :, pl.ds(pl.multiple_of(c * LANES, LANES), LANES)] = acc
        return 0

    lax.fori_loop(0, nsn * chunks, chunk, 0)


def build_kernels(count_ref, pts_ref, k_ref, nsn, width):
    step = 64

    def one(s, _):
        first = width - count_ref[s]
        rows = pts_ref[s]
        cols = jnp.transpose(rows)
        for r in range(width // step):
            lo = r * step
            base = lo // LANES * LANES
            wide = width - base
            square = None
            for c in range(3):
                diff = cols[lo : lo + step, c : c + 1] - rows[c : c + 1, base:]
                square = diff * diff if square is None else square + diff * diff
            dist = jnp.sqrt(square) * (math.sqrt(3.0) / LENGTH_SCALE)
            kern = (1.0 + dist) * jnp.exp(-dist)
            p = lo + lax.broadcasted_iota(jnp.int32, (step, wide), 0)
            q = base + lax.broadcasted_iota(jnp.int32, (step, wide), 1)
            kern = jnp.where(jnp.minimum(p, q) >= first, kern, 0.0)
            kern = kern + jnp.where(p == q, jnp.where(p >= first, NUGGET, 1.0), 0.0)
            k_ref[s, lo : lo + step, base:] = kern
        return 0

    lax.fori_loop(0, nsn, one, 0)


def leaf(k_ref, work_ref, inv_ref, t, nsn):
    row = lax.broadcasted_iota(jnp.int32, (MEMB, LANES), 0)
    lane = lax.broadcasted_iota(jnp.int32, (MEMB, LANES), 1)
    lane_one = lax.broadcasted_iota(jnp.int32, (1, LANES), 1)
    lo = t * MEMB
    base = lo // LANES * LANES
    eye = (row + MEMB == lane).astype(F32)

    def load(s, _):
        tile = k_ref[s, lo : lo + MEMB, base : base + LANES]
        if lo != base:
            tile = pltpu.roll(tile, MEMB, 1)
        work_ref[s] = jnp.where(lane < MEMB, tile, eye)
        return 0

    lax.fori_loop(0, nsn, load, 0)

    for half in range(2):
        top = half * (MEMB // 2)
        tall = MEMB - top

        def pivot(k, _):
            hit = lane[:tall] == k
            below = row[:tall] + top > k
            nows = [work_ref[s, pl.ds(k, 1), :] for s in range(nsn)]
            pivs = [jnp.sum(jnp.where(lane_one == k, now, 0.0), axis=1, keepdims=True) for now in nows]
            nows = [now / piv for now, piv in zip(nows, pivs)]
            for s in range(nsn):
                full = work_ref[s, top:]
                col = jnp.sum(jnp.where(hit, full, 0.0), axis=1, keepdims=True)
                work_ref[s, top:] = full - jnp.where(below, col, 0.0) * nows[s]
            return 0

        lax.fori_loop(top, top + MEMB // 2, pivot, 0)

    def finish(s, _):
        full = work_ref[s]
        diag = jnp.sum(jnp.where(row == lane, full, 0.0), axis=1, keepdims=True)
        inv_ref[t, s] = pltpu.roll(full, MEMB, 1)[:, :MEMB] * lax.rsqrt(diag)
        return 0

    lax.fori_loop(0, nsn, finish, 0)


def update(k_ref, inv_ref, t, nsn, width):
    lo = t * MEMB
    after = lo + MEMB
    base = after // LANES * LANES

    group = 4

    def some(n, _):
        sets = [n * group + u for u in range(group)]
        rows = [dot3(inv_ref[t, s], k_ref[s, lo:after, base:]) for s in sets]
        parts = [split(x) for x in rows]
        left = [jnp.concatenate([high, low, high], axis=0) for high, low in parts]
        right = [jnp.concatenate([high, high, low], axis=0) for high, low in parts]
        for r in range(base, width, LANES):
            skip = MEMB if r == base and base != after else 0
            pieces = [
                dot(x[:, r - base : r - base + LANES], y[:, r - base :], ((0,), (0,)))[skip:]
                for x, y in zip(left, right)
            ]
            fresh = [k_ref[s, r + skip : r + LANES, r:] - piece for s, piece in zip(sets, pieces)]
            for s, value in zip(sets, fresh):
                k_ref[s, r + skip : r + LANES, r:] = value
        for s, value in zip(sets, rows):
            k_ref[s, lo:after, base:] = value
        return 0

    lax.fori_loop(0, nsn // group, some, 0)


def back(k_ref, inv_ref, target_ref, out_ref, rest_ref, nsn, width):
    stages = width // MEMB

    group = 4

    def some(n, _):
        sets = [n * group + u for u in range(group)]
        nows = [jnp.transpose(inv_ref[stages - 1, s]) for s in sets]
        for u in range(group):
            rest_ref[u, width - MEMB :] = nows[u]
        for j in range(stages - 1, 0, -1):
            lo = j * MEMB
            pieces = [dot3(k_ref[s, :lo, lo : lo + MEMB], now) for s, now in zip(sets, nows)]
            for u in range(group):
                if j == stages - 1:
                    rest_ref[u, :lo] = -pieces[u]
                else:
                    rest_ref[u, :lo] = rest_ref[u, :lo] - pieces[u]
            nows = [dot3(inv_ref[j - 1, s], rest_ref[u, lo - MEMB : lo], ((0,), (0,))) for u, s in enumerate(sets)]
            for u in range(group):
                rest_ref[u, lo - MEMB : lo] = nows[u]
        for u, s in enumerate(sets):
            out_ref[target_ref[s]] = jnp.transpose(rest_ref[u])
        return 0

    lax.fori_loop(0, nsn // group, some, 0)


def factor_kernel(index_ref, count_ref, target_ref, table_ref, out_ref, pts_ref, k_ref, work_ref, inv_ref, rest_ref):
    nsn, width = index_ref.shape
    stages = width // MEMB
    gather_points(table_ref, index_ref, pts_ref, nsn, width)
    build_kernels(count_ref, pts_ref, k_ref, nsn, width)
    for t in range(stages):
        leaf(k_ref, work_ref, inv_ref, t, nsn)
        if t < stages - 1:
            update(k_ref, inv_ref, t, nsn, width)
    back(k_ref, inv_ref, target_ref, out_ref, rest_ref, nsn, width)


def factor_all(table, wanted, count, target, slots):
    nsn, width = wanted.shape
    smem = pl.BlockSpec(memory_space=pltpu.SMEM)
    vmem = pl.BlockSpec(memory_space=pltpu.VMEM)
    return pl.pallas_call(
        factor_kernel,
        out_shape=jax.ShapeDtypeStruct((slots, MEMB, width), F32),
        in_specs=[smem, smem, smem, vmem],
        out_specs=vmem,
        scratch_shapes=[
            pltpu.VMEM((nsn, 8, width), F32),
            pltpu.VMEM((nsn, width, width), F32),
            pltpu.VMEM((nsn, MEMB, LANES), F32),
            pltpu.VMEM((width // MEMB, nsn, MEMB, MEMB), F32),
            pltpu.VMEM((4, width, MEMB), F32),
        ],
        compiler_params=pltpu.CompilerParams(vmem_limit_bytes=50 * 1024 * 1024),
        name="factor",
    )(wanted, count, target, table)


def place_kernel(spot_ref, got_ref, out_ref):
    nlocal = out_ref.shape[0]
    for i in range(got_ref.shape[0]):
        @pl.when(spot_ref[i] < nlocal)
        def _():
            out_ref[spot_ref[i]] = got_ref[i]


def place_all(got, spot, nlocal):
    vmem = pl.BlockSpec(memory_space=pltpu.VMEM)
    return pl.pallas_call(
        place_kernel,
        out_shape=jax.ShapeDtypeStruct((nlocal,) + got.shape[1:], F32),
        in_specs=[pl.BlockSpec(memory_space=pltpu.SMEM), vmem],
        out_specs=vmem,
        compiler_params=pltpu.CompilerParams(vmem_limit_bytes=16 * 1024 * 1024),
        name="place",
    )(spot, got)


def body(coords_fine, coords_coarse, set_index, counts, morton_slot):
    width = set_index.shape[-1]
    ends = lax.axis_size("slab") - 1
    fine = lax.all_gather(coords_fine, "inner", axis=1, tiled=True)
    below = lax.ppermute(coords_coarse, "slab", [(i, i + 1) for i in range(ends)])
    above = lax.ppermute(coords_coarse, "slab", [(i + 1, i) for i in range(ends)])
    table = jnp.concatenate([fine, below, coords_coarse, above], axis=1)
    table = jnp.pad(table, ((0, 5), (0, 0)))
    wanted = set_index.reshape(-1, width)
    count_here = counts.reshape(-1)
    places = morton_slot.reshape(-1)
    nlocal = wanted.shape[0]
    peers = lax.axis_size("inner")
    capacity = max(1, nlocal // peers)
    slots = peers * capacity
    owner = places // nlocal
    spot = places % nlocal
    order = jnp.arange(nlocal, dtype=jnp.int32)
    earlier = (owner[:, None] == owner[None, :]) & (order[None, :] < order[:, None])
    target = owner * capacity + jnp.sum(earlier.astype(jnp.int32), axis=1)
    hits = target[None, :] == jnp.arange(slots, dtype=jnp.int32)[:, None]
    send_spot = nlocal + jnp.sum(jnp.where(hits, spot[None, :] - nlocal, 0), axis=1)
    got_spot = lax.all_to_all(send_spot, "inner", split_axis=0, concat_axis=0, tiled=True)
    blocks = factor_all(table, wanted, count_here, target, slots)
    got_blocks = lax.all_to_all(blocks, "inner", split_axis=0, concat_axis=0, tiled=True)
    result = place_all(got_blocks, got_spot, nlocal)
    return result.reshape(1, 1, nlocal, MEMB, width)


def solution(mesh):
    placed = (
        P(None, ("slab", "inner")),
        P(None, "slab"),
        P("slab", None, "inner", None),
        P("slab", None, "inner"),
        P("slab", None, "inner"),
    )
    return jax.shard_map(
        body,
        mesh=mesh,
        in_specs=placed,
        out_specs=P("slab", "inner", None, None, None),
        check_vma=False,
    )
```

```python
import math

import jax
import jax.numpy as jnp
from jax import lax
from jax.experimental import pallas as pl
from jax.experimental.pallas import tpu as pltpu
from jax.sharding import PartitionSpec as P

MEMB = 64
LENGTH_SCALE = 0.2
NUGGET = 0.5
LANES = 128
F32 = jnp.float32
BF16 = jnp.bfloat16


def split(x):
    high = x.astype(BF16)
    return high, (x - high.astype(F32)).astype(BF16)


def dot(a, b, dims=((1,), (0,))):
    return lax.dot_general(a, b, (dims, ((), ())), preferred_element_type=F32)


def dot3(a, b, dims=((1,), (0,))):
    ah, al = split(a)
    bh, bl = split(b)
    return dot(ah, bh, dims) + (dot(ah, bl, dims) + dot(al, bh, dims))


def gather_points(table_ref, index_ref, pts_ref, nsn, width):
    lane = lax.broadcasted_iota(jnp.int32, (8, LANES), 1)
    chunks = width // LANES

    def chunk(n, _):
        s = n // chunks
        c = n % chunks
        acc = jnp.zeros((8, LANES), F32)
        for p in range(LANES):
            number = index_ref[s, c * LANES + p]
            start = pl.multiple_of((number >> 7) * LANES, LANES)
            tile = table_ref[:, pl.ds(start, LANES)]
            tile = pltpu.roll(tile, (p - number) & (LANES - 1), 1)
            acc = jnp.where(lane == p, tile, acc)
        pts_ref[s, :, pl.ds(pl.multiple_of(c * LANES, LANES), LANES)] = acc
        return 0

    lax.fori_loop(0, nsn * chunks, chunk, 0)


def build_kernels(count_ref, pts_ref, k_ref, nsn, width):
    step = 64

    def one(s, _):
        first = width - count_ref[s]
        rows = pts_ref[s]
        cols = jnp.transpose(rows)
        for r in range(width // step):
            lo = r * step
            base = lo // LANES * LANES
            wide = width - base
            square = None
            for c in range(3):
                diff = cols[lo : lo + step, c : c + 1] - rows[c : c + 1, base:]
                square = diff * diff if square is None else square + diff * diff
            dist = jnp.sqrt(square) * (math.sqrt(3.0) / LENGTH_SCALE)
            kern = (1.0 + dist) * jnp.exp(-dist)
            p = lo + lax.broadcasted_iota(jnp.int32, (step, wide), 0)
            q = base + lax.broadcasted_iota(jnp.int32, (step, wide), 1)
            kern = jnp.where(jnp.minimum(p, q) >= first, kern, 0.0)
            kern = kern + jnp.where(p == q, jnp.where(p >= first, NUGGET, 1.0), 0.0)
            k_ref[s, lo : lo + step, base:] = kern
        return 0

    lax.fori_loop(0, nsn, one, 0)


def leaf(k_ref, work_ref, inv_ref, t, nsn):
    row = lax.broadcasted_iota(jnp.int32, (MEMB, LANES), 0)
    lane = lax.broadcasted_iota(jnp.int32, (MEMB, LANES), 1)
    lane_one = lax.broadcasted_iota(jnp.int32, (1, LANES), 1)
    lo = t * MEMB
    base = lo // LANES * LANES
    eye = (row + MEMB == lane).astype(F32)

    def load(s, _):
        tile = k_ref[s, lo : lo + MEMB, base : base + LANES]
        if lo != base:
            tile = pltpu.roll(tile, MEMB, 1)
        work_ref[s] = jnp.where(lane < MEMB, tile, eye)
        return 0

    lax.fori_loop(0, nsn, load, 0)

    for part in range(4):
        top = part * (MEMB // 4)
        tall = MEMB - top

        def pivot(k, _):
            hit = lane[:tall] == k
            below = row[:tall] + top > k
            nows = [work_ref[s, pl.ds(k, 1), :] for s in range(nsn)]
            pivs = [jnp.sum(jnp.where(lane_one == k, now, 0.0), axis=1, keepdims=True) for now in nows]
            nows = [now / piv for now, piv in zip(nows, pivs)]
            for s in range(nsn):
                full = work_ref[s, top:]
                col = jnp.sum(jnp.where(hit, full, 0.0), axis=1, keepdims=True)
                work_ref[s, top:] = full - jnp.where(below, col, 0.0) * nows[s]
            return 0

        lax.fori_loop(top, top + MEMB // 4, pivot, 0)

    def finish(s, _):
        full = work_ref[s]
        diag = jnp.sum(jnp.where(row == lane, full, 0.0), axis=1, keepdims=True)
        inv_ref[t, s] = pltpu.roll(full, MEMB, 1)[:, :MEMB] * lax.rsqrt(diag)
        return 0

    lax.fori_loop(0, nsn, finish, 0)


def update(k_ref, inv_ref, t, nsn, width):
    lo = t * MEMB
    after = lo + MEMB
    base = after // LANES * LANES

    group = 4

    def some(n, _):
        sets = [n * group + u for u in range(group)]
        rows = [dot3(inv_ref[t, s], k_ref[s, lo:after, base:]) for s in sets]
        parts = [split(x) for x in rows]
        left = [jnp.concatenate([high, low, high], axis=0) for high, low in parts]
        right = [jnp.concatenate([high, high, low], axis=0) for high, low in parts]
        for r in range(base, width, LANES):
            skip = MEMB if r == base and base != after else 0
            pieces = [
                dot(x[:, r - base : r - base + LANES], y[:, r - base :], ((0,), (0,)))[skip:]
                for x, y in zip(left, right)
            ]
            fresh = [k_ref[s, r + skip : r + LANES, r:] - piece for s, piece in zip(sets, pieces)]
            for s, value in zip(sets, fresh):
                k_ref[s, r + skip : r + LANES, r:] = value
        for s, value in zip(sets, rows):
            k_ref[s, lo:after, base:] = value
        return 0

    lax.fori_loop(0, nsn // group, some, 0)


def back(k_ref, inv_ref, target_ref, out_ref, rest_ref, nsn, width):
    stages = width // MEMB

    group = 4

    def some(n, _):
        sets = [n * group + u for u in range(group)]
        nows = [jnp.transpose(inv_ref[stages - 1, s]) for s in sets]
        for u in range(group):
            rest_ref[u, width - MEMB :] = nows[u]
        for j in range(stages - 1, 0, -1):
            lo = j * MEMB
            pieces = [dot3(k_ref[s, :lo, lo : lo + MEMB], now) for s, now in zip(sets, nows)]
            for u in range(group):
                if j == stages - 1:
                    rest_ref[u, :lo] = -pieces[u]
                else:
                    rest_ref[u, :lo] = rest_ref[u, :lo] - pieces[u]
            nows = [dot3(inv_ref[j - 1, s], rest_ref[u, lo - MEMB : lo], ((0,), (0,))) for u, s in enumerate(sets)]
            for u in range(group):
                rest_ref[u, lo - MEMB : lo] = nows[u]
        for u, s in enumerate(sets):
            out_ref[target_ref[s]] = jnp.transpose(rest_ref[u])
        return 0

    lax.fori_loop(0, nsn // group, some, 0)


def factor_kernel(index_ref, count_ref, target_ref, table_ref, out_ref, pts_ref, k_ref, work_ref, inv_ref, rest_ref):
    nsn, width = index_ref.shape
    stages = width // MEMB
    gather_points(table_ref, index_ref, pts_ref, nsn, width)
    build_kernels(count_ref, pts_ref, k_ref, nsn, width)
    for t in range(stages):
        leaf(k_ref, work_ref, inv_ref, t, nsn)
        if t < stages - 1:
            update(k_ref, inv_ref, t, nsn, width)
    back(k_ref, inv_ref, target_ref, out_ref, rest_ref, nsn, width)


def factor_all(table, wanted, count, target, slots):
    nsn, width = wanted.shape
    smem = pl.BlockSpec(memory_space=pltpu.SMEM)
    vmem = pl.BlockSpec(memory_space=pltpu.VMEM)
    return pl.pallas_call(
        factor_kernel,
        out_shape=jax.ShapeDtypeStruct((slots, MEMB, width), F32),
        in_specs=[smem, smem, smem, vmem],
        out_specs=vmem,
        scratch_shapes=[
            pltpu.VMEM((nsn, 8, width), F32),
            pltpu.VMEM((nsn, width, width), F32),
            pltpu.VMEM((nsn, MEMB, LANES), F32),
            pltpu.VMEM((width // MEMB, nsn, MEMB, MEMB), F32),
            pltpu.VMEM((4, width, MEMB), F32),
        ],
        compiler_params=pltpu.CompilerParams(vmem_limit_bytes=50 * 1024 * 1024),
        name="factor",
    )(wanted, count, target, table)


def place_kernel(spot_ref, got_ref, out_ref):
    nlocal = out_ref.shape[0]
    for i in range(got_ref.shape[0]):
        @pl.when(spot_ref[i] < nlocal)
        def _():
            out_ref[spot_ref[i]] = got_ref[i]


def place_all(got, spot, nlocal):
    vmem = pl.BlockSpec(memory_space=pltpu.VMEM)
    return pl.pallas_call(
        place_kernel,
        out_shape=jax.ShapeDtypeStruct((nlocal,) + got.shape[1:], F32),
        in_specs=[pl.BlockSpec(memory_space=pltpu.SMEM), vmem],
        out_specs=vmem,
        compiler_params=pltpu.CompilerParams(vmem_limit_bytes=16 * 1024 * 1024),
        name="place",
    )(spot, got)


def body(coords_fine, coords_coarse, set_index, counts, morton_slot):
    width = set_index.shape[-1]
    ends = lax.axis_size("slab") - 1
    fine = lax.all_gather(coords_fine, "inner", axis=1, tiled=True)
    below = lax.ppermute(coords_coarse, "slab", [(i, i + 1) for i in range(ends)])
    above = lax.ppermute(coords_coarse, "slab", [(i + 1, i) for i in range(ends)])
    table = jnp.concatenate([fine, below, coords_coarse, above], axis=1)
    table = jnp.pad(table, ((0, 5), (0, 0)))
    wanted = set_index.reshape(-1, width)
    count_here = counts.reshape(-1)
    places = morton_slot.reshape(-1)
    nlocal = wanted.shape[0]
    peers = lax.axis_size("inner")
    capacity = max(1, nlocal // peers)
    slots = peers * capacity
    owner = places // nlocal
    spot = places % nlocal
    order = jnp.arange(nlocal, dtype=jnp.int32)
    earlier = (owner[:, None] == owner[None, :]) & (order[None, :] < order[:, None])
    target = owner * capacity + jnp.sum(earlier.astype(jnp.int32), axis=1)
    hits = target[None, :] == jnp.arange(slots, dtype=jnp.int32)[:, None]
    send_spot = nlocal + jnp.sum(jnp.where(hits, spot[None, :] - nlocal, 0), axis=1)
    got_spot = lax.all_to_all(send_spot, "inner", split_axis=0, concat_axis=0, tiled=True)
    blocks = factor_all(table, wanted, count_here, target, slots)
    got_blocks = lax.all_to_all(blocks, "inner", split_axis=0, concat_axis=0, tiled=True)
    result = place_all(got_blocks, got_spot, nlocal)
    return result.reshape(1, 1, nlocal, MEMB, width)


def solution(mesh):
    placed = (
        P(None, ("slab", "inner")),
        P(None, "slab"),
        P("slab", None, "inner", None),
        P("slab", None, "inner"),
        P("slab", None, "inner"),
    )
    return jax.shard_map(
        body,
        mesh=mesh,
        in_specs=placed,
        out_specs=P("slab", "inner", None, None, None),
        check_vma=False,
    )
```
